512 devices in a mesh: row: 16 (over x_hi, z), col: 16 (over y, x_lo), dp: 2 (over core).
Axes of the slice: x: 4 (x_hi: 2, x_lo: 2; x = x_hi * 2 + x_lo), y: 8, z: 8, core: 2. Of those that a mesh axis runs over, the one named last changes fastest.
Arguments:
- tokens: bfloat16 [512, 8192], P(('col', 'dp'), 'row'), may hold values from -6 to 6
- grad_out: bfloat16 [512, 8192], P(('col', 'dp'), 'row'), may hold values from -1.1953125 to 1.1953125
- gate_weight: bfloat16 [8192, 16384], P('row', 'col'), may hold values from -0.0625 to 0.0625
- up_weight: bfloat16 [8192, 16384], P('row', 'col'), may hold values from -0.0625 to 0.0625
- down_weight: bfloat16 [16384, 8192], P('col', 'row'), may hold values from -0.046875 to 0.046875
Outputs:
- grad_tokens: bfloat16 [512, 8192], P(('col', 'dp'), 'row')
- grad_gate: bfloat16 [8192, 16384], P('row', ('col', 'dp'))
- grad_up: bfloat16 [8192, 16384], P('row', ('col', 'dp'))
- grad_down: bfloat16 [16384, 8192], P(('col', 'dp'), 'row')
The draws below stay inside these ranges and needn't reach their ends.
All inputs are finite; a program needn't handle non-finite values.
Results may differ from the reference program's by a relative error of at most 0.0049.
Values may be sent and summed in bfloat16 or wider, within the bound.
No kernel may reach another device: no remote copies, remote signals or barrier semaphores. Data moves between devices by JAX's collectives and lax.ppermute only.
A program may use at most 64 MiB of HBM per device.

```python
import jax
import jax.numpy as jnp
from jax import lax

D = 8192
FFW = 16384
TOKENS = 512


def level_of(own_key, shape, shards, least, high):
    def one(dim, shards_of):
        heights = jax.random.uniform(jax.random.fold_in(jax.random.fold_in(own_key, 6), dim), (shards_of,), jnp.float32, least / len(shards), high / len(shards))
        return jnp.repeat(jnp.exp(heights), shape[dim] // shards_of).reshape((-1,) + (1,) * (len(shape) - dim - 1))

    factor_of = one(*shards[0])
    for cut in shards[1:]:
        factor_of = factor_of * one(*cut)
    return factor_of


def centred(own_key, shape, scale, limit, shards=(), held_as=jnp.bfloat16):
    entries = scale * jax.random.normal(own_key, shape, jnp.float32)
    if shards:
        entries = entries * level_of(own_key, shape, shards, -0.22, 0.18)
    return jnp.clip(entries, -limit, limit).astype(held_as)


def setup_inputs(seed: int = 0) -> dict:
    seeds = jax.random.split(jax.random.key(seed), 6)
    return {
        "tokens": centred(seeds[0], (TOKENS, D), 1.0, 6.0, ((0, 32), (1, 16))),
        "grad_out": centred(seeds[1], (TOKENS, D), 0.2, 1.1953125, ((0, 32), (1, 16))),
        "gate_weight": centred(seeds[2], (D, FFW), D ** -0.5, 0.0625, ((0, 16), (1, 16))),
        "up_weight": centred(seeds[3], (D, FFW), D ** -0.5, 0.0625, ((0, 16), (1, 16))),
        "down_weight": centred(seeds[4], (FFW, D), FFW ** -0.5, 0.046875, ((0, 16), (1, 16))),
    }


def reference(tokens, grad_out, gate_weight, up_weight, down_weight):
    contract_last = (((1,), (1,)), ((), ()))
    contract_first = (((0,), (0,)), ((), ()))
    gate = jnp.dot(tokens, gate_weight, preferred_element_type=jnp.float32)
    up = jnp.dot(tokens, up_weight, preferred_element_type=jnp.float32)
    grad_hidden = lax.dot_general(grad_out, down_weight, contract_last, preferred_element_type=jnp.float32)
    sig = jax.nn.sigmoid(gate)
    hidden = (gate * sig * up).astype(jnp.bfloat16)
    grad_g = (grad_hidden * up * sig * (1.0 + gate * (1.0 - sig))).astype(jnp.bfloat16)
    grad_u = (grad_hidden * gate * sig).astype(jnp.bfloat16)
    grad_tokens = lax.dot_general(grad_g, gate_weight, contract_last, preferred_element_type=jnp.float32)
    grad_tokens = grad_tokens + lax.dot_general(grad_u, up_weight, contract_last, preferred_element_type=jnp.float32)
    grad_gate = lax.dot_general(tokens, grad_g, contract_first, preferred_element_type=jnp.float32)
    grad_up = lax.dot_general(tokens, grad_u, contract_first, preferred_element_type=jnp.float32)
    grad_down = lax.dot_general(hidden, grad_out, contract_first, preferred_element_type=jnp.float32)
    return (grad_tokens.astype(jnp.bfloat16), grad_gate.astype(jnp.bfloat16),
            grad_up.astype(jnp.bfloat16), grad_down.astype(jnp.bfloat16))
```

```python
import jax
import jax.numpy as jnp
from jax import lax
from jax.sharding import Mesh, PartitionSpec as P

ROW, COL = ("x_hi", "z"), ("y", "x_lo")
LAST = (((1,), (1,)), ((), ()))
FIRST = (((0,), (0,)), ((), ()))
SWAP = [(0, 1), (1, 0)]
f32, bf16 = jnp.float32, jnp.bfloat16


def swiglu_back(gate, up, grad_hidden):
    sig = jax.nn.sigmoid(gate)
    hidden = (gate * sig * up).astype(bf16)
    grad_g = (grad_hidden * up * sig * (1.0 + gate * (1.0 - sig))).astype(bf16)
    grad_u = (grad_hidden * gate * sig).astype(bf16)
    return hidden, grad_g, grad_u


def gather(x, axis, n):
    rows, cols = x.shape
    copies = jnp.broadcast_to(x[None], (n, rows, cols))
    return lax.all_to_all(copies, axis, 0, 0, tiled=True).reshape(n * rows, cols)


def scatter_sum(x, axis, n):
    rows, cols = x.shape
    blocks = lax.all_to_all(x.reshape(n, rows // n, cols), axis, 0, 0, tiled=True)
    return jnp.sum(blocks.astype(f32), axis=0)


def body(tokens, grad_out, gate_weight, up_weight, down_weight):
    x_hi, dp = lax.axis_index("x_hi"), lax.axis_index("dp")
    keep, send = dp * 512 + x_hi * 256, dp * 512 + (1 - x_hi) * 256

    def columns(at):
        return jnp.concatenate(
            [lax.dynamic_slice(w, (0, at), (512, 256)) for w in (gate_weight, up_weight)], axis=1
        )

    gu_keep, gu_send = columns(keep), columns(send)
    down_keep = lax.dynamic_slice(down_weight, (keep, 0), (256, 512))
    down_send = lax.dynamic_slice(down_weight, (send, 0), (256, 512))

    own_in = gather(tokens, COL, 16)
    own_grad = gather(grad_out, COL, 16)
    both_in = jnp.concatenate([own_in, lax.ppermute(own_in, "dp", SWAP)])
    both_grad = jnp.concatenate([own_grad, lax.ppermute(own_grad, "dp", SWAP)])

    def row_sum(x, w_keep, w_send, dims):
        sent = lax.dot_general(x, w_send, dims, preferred_element_type=f32).astype(bf16)
        got = lax.ppermute(sent, "x_hi", SWAP)
        part = lax.dot_general(x, w_keep, dims, preferred_element_type=f32) + got.astype(f32)
        return scatter_sum(part.astype(bf16), "z", 8)

    gu = row_sum(both_in, gu_keep, gu_send, (((1,), (0,)), ((), ())))
    grad_hidden = row_sum(both_grad, down_keep, down_send, LAST)
    hidden, grad_g, grad_u = swiglu_back(gu[:, :256], gu[:, 256:], grad_hidden)

    own_gu = gather(jnp.concatenate([grad_g, grad_u], axis=1), "z", 8)
    own_h = gather(hidden, "z", 8)
    far_gu = lax.ppermute(own_gu, "x_hi", SWAP)
    far_h = lax.ppermute(own_h, "x_hi", SWAP)

    total = lax.dot_general(own_gu, gu_keep, LAST, preferred_element_type=f32)
    total = total + lax.dot_general(far_gu, gu_send, LAST, preferred_element_type=f32)
    panel = total[:256] + lax.ppermute(total[256:], "dp", SWAP)
    grad_tokens = scatter_sum(panel.astype(bf16), COL, 16).astype(bf16)

    def both_halves(own, far):
        first = x_hi == 0
        return jnp.concatenate([jnp.where(first, own, far), jnp.where(first, far, own)], axis=1)

    all_g = both_halves(own_gu[:, :256], far_gu[:, :256])
    all_u = both_halves(own_gu[:, 256:], far_gu[:, 256:])
    all_h = both_halves(own_h, far_h)
    grad_gate = lax.dot_general(both_in, all_g, FIRST, preferred_element_type=f32)
    grad_up = lax.dot_general(both_in, all_u, FIRST, preferred_element_type=f32)
    grad_down = lax.dot_general(all_h, both_grad, FIRST, preferred_element_type=f32)
    return grad_tokens, grad_gate.astype(bf16), grad_up.astype(bf16), grad_down.astype(bf16)


def solution(mesh):
    fine = Mesh(mesh.devices.reshape(2, 8, 8, 2, 2), ("x_hi", "z", "y", "x_lo", "dp"))
    in_specs = (
        P(COL + ("dp",), ROW),
        P(COL + ("dp",), ROW),
        P(ROW, COL),
        P(ROW, COL),
        P(COL, ROW),
    )
    out_specs = (
        P(COL + ("dp",), ROW),
        P(ROW, COL + ("dp",)),
        P(ROW, COL + ("dp",)),
        P(COL + ("dp",), ROW),
    )
    return jax.shard_map(body, mesh=fine, in_specs=in_specs, out_specs=out_specs, check_vma=False)
```

```python
import jax
import jax.numpy as jnp
from jax import lax
from jax.experimental import pallas as pl
from jax.experimental.pallas import tpu as pltpu
from jax.sharding import Mesh, PartitionSpec as P

ROW, COL = ("x_hi", "z"), ("y", "x_lo")
PLAIN = (((1,), (0,)), ((), ()))
LAST = (((1,), (1,)), ((), ()))
FIRST = (((0,), (0,)), ((), ()))
SWAP = [(0, 1), (1, 0)]
f32, bf16 = jnp.float32, jnp.bfloat16


def swiglu_back(gate, up, grad_hidden):
    sig = jax.nn.sigmoid(gate)
    hidden = (gate * sig * up).astype(bf16)
    grad_g = (grad_hidden * up * sig * (1.0 + gate * (1.0 - sig))).astype(bf16)
    grad_u = (grad_hidden * gate * sig).astype(bf16)
    return hidden, grad_g, grad_u


def dot(a, b, dims):
    return lax.dot_general(a, b, dims, preferred_element_type=f32)


def gather(x, axis, n):
    rows, cols = x.shape
    copies = jnp.broadcast_to(x[None], (n, rows, cols))
    return lax.all_to_all(copies, axis, 0, 0, tiled=True).reshape(n * rows, cols)


def scatter_sum(x, axis, n):
    rows, cols = x.shape
    blocks = lax.all_to_all(x.reshape(n, rows // n, cols), axis, 0, 0, tiled=True)
    return jnp.sum(blocks.astype(f32), axis=0)


def gate_up_grads_kernel(x_hi, own, other, own_gu, far_gu, other_own, other_far, gate_ref, up_ref):
    def part(mine, others):
        total = dot(own[...], mine[:, :512], FIRST) + dot(other[...], others[...], FIRST)
        gate_ref[...] = total[:, :256].astype(bf16)
        up_ref[...] = total[:, 256:].astype(bf16)

    pl.when(pl.program_id(0) == 0)(lambda: part(own_gu, other_own))
    pl.when(pl.program_id(0) == 1)(lambda: part(far_gu, other_far))


def gate_up_grads(x_hi, own, other, own_gu, far_gu, other_own, other_far):
    whole = lambda shape: pl.BlockSpec(shape, lambda q, at: (0, 0))
    out = pl.BlockSpec((512, 256), lambda q, at: (0, at[0] ^ q))
    shape = jax.ShapeDtypeStruct((512, 512), bf16)
    return pl.pallas_call(
        gate_up_grads_kernel,
        out_shape=(shape, shape),
        grid_spec=pltpu.PrefetchScalarGridSpec(
            num_scalar_prefetch=1,
            grid=(2,),
            in_specs=[whole((256, 512)), whole((256, 512)), whole((256, 1024)), whole((256, 1024)),
                      whole((256, 512)), whole((256, 512))],
            out_specs=(out, out),
        ),
        compiler_params=pltpu.CompilerParams(vmem_limit_bytes=24 * 2**20),
        cost_estimate=pl.CostEstimate(flops=2 * 512**3 * 2, bytes_accessed=4 * 2**20, transcendentals=0),
    )(x_hi, own, other, own_gu, far_gu, other_own, other_far)


def down_grads_kernel(at, own, other, h, out_ref):
    total = dot(h[:, :256], own[...], FIRST) + dot(h[:, 256:], other[...], FIRST)
    out_ref[...] = total.astype(bf16)


def down_grads(at, own, other, h):
    half = lambda q, at: (0, 1)
    return pl.pallas_call(
        down_grads_kernel,
        out_shape=jax.ShapeDtypeStruct((512, 512), bf16),
        grid_spec=pltpu.PrefetchScalarGridSpec(
            num_scalar_prefetch=1,
            grid=(2,),
            in_specs=[pl.BlockSpec((256, 512), half), pl.BlockSpec((256, 512), half),
                      pl.BlockSpec((256, 512), lambda q, at: (0, q))],
            out_specs=pl.BlockSpec((256, 512), lambda q, at: (at[0] ^ q, 0)),
        ),
        compiler_params=pltpu.CompilerParams(vmem_limit_bytes=24 * 2**20),
        cost_estimate=pl.CostEstimate(flops=2 * 512**3, bytes_accessed=2 * 2**20, transcendentals=0),
    )(at, own, other, h)


def body(tokens, grad_out, gate_weight, up_weight, down_weight):
    x_hi, dp = lax.axis_index("x_hi"), lax.axis_index("dp")
    def quarter(x, core, side):
        return lax.dynamic_slice(x, (0, core * 512 + side * 256), (x.shape[0], 256))

    def gate_up(side):
        return jnp.concatenate(
            [quarter(w, core, side) for core in (dp, 1 - dp) for w in (gate_weight, up_weight)], axis=1
        )

    gu_keep, gu_send = gate_up(x_hi), gate_up(1 - x_hi)
    own = gather(jnp.concatenate([tokens, grad_out], axis=1), COL, 16)
    own, gu_keep, gu_send = lax.optimization_barrier((own, gu_keep, gu_send))
    own_in, own_grad = own[:, :512], own[:, 512:]

    got = lax.ppermute(dot(own_in, gu_send, PLAIN).astype(bf16), "x_hi", SWAP)
    gh_part = scatter_sum(dot(own_grad, down_weight, LAST).astype(bf16), "z", 8)

    def grad_hidden(side):
        return jnp.concatenate([quarter(gh_part, dp, side), quarter(gh_part, 1 - dp, side)], axis=1)

    gh = grad_hidden(x_hi) + lax.ppermute(grad_hidden(1 - x_hi), "x_hi", SWAP)
    other = lax.ppermute(own, "dp", SWAP)
    kept = lax.optimization_barrier(dot(own_in, gu_keep, PLAIN))
    got, other = lax.optimization_barrier((got, other))
    gu = scatter_sum((kept + got.astype(f32)).astype(bf16), "z", 8)
    gate = jnp.concatenate([gu[:, :256], gu[:, 512:768]], axis=1)
    up = jnp.concatenate([gu[:, 256:512], gu[:, 768:]], axis=1)
    hidden, g, u = swiglu_back(gate, up, gh)

    own_gu = gather(jnp.concatenate([g[:, :256], u[:, :256], g[:, 256:], u[:, 256:]], axis=1), "z", 8)
    hidden = jnp.concatenate([hidden[:, :256], lax.ppermute(hidden[:, 256:], "dp", SWAP)], axis=1)
    hidden = jnp.concatenate([hidden, lax.ppermute(hidden, "x_hi", SWAP)], axis=1)
    own_gu, hidden = lax.optimization_barrier((own_gu, hidden))
    all_h = gather(hidden, "z", 8)

    far_gu = lax.ppermute(own_gu, "x_hi", SWAP)
    other_own = lax.ppermute(own_gu[:, 512:], "dp", SWAP)
    far_gu, other_own = lax.optimization_barrier((far_gu, other_own))
    kept = lax.optimization_barrier(dot(own_gu, gu_keep, LAST))
    panel = (kept + dot(far_gu, gu_send, LAST)).astype(bf16)
    panel, far_gu = lax.optimization_barrier((panel, far_gu))
    grad_tokens = scatter_sum(panel, COL, 16).astype(bf16)

    other_far = lax.ppermute(far_gu[:, 512:], "dp", SWAP)
    at = x_hi.astype(jnp.int32)[None]
    grad_gate, grad_up = gate_up_grads(
        at, own, other, own_gu, far_gu, other_own, other_far
    )
    grad_down = down_grads(at, own, other, all_h)
    return grad_tokens, grad_gate, grad_up, grad_down


def solution(mesh):
    fine = Mesh(mesh.devices.reshape(2, 8, 8, 2, 2), ("x_hi", "z", "y", "x_lo", "dp"))
    in_specs = (
        P(COL + ("dp",), ROW),
        P(COL + ("dp",), ROW),
        P(ROW, COL),
        P(ROW, COL),
        P(COL, ROW),
    )
    out_specs = (
        P(COL + ("dp",), ROW),
        P(ROW, COL + ("dp",)),
        P(ROW, COL + ("dp",)),
        P(COL + ("dp",), ROW),
    )
    return jax.shard_map(body, mesh=fine, in_specs=in_specs, out_specs=out_specs, check_vma=False)
```

```python
import jax
import jax.numpy as jnp
from jax import lax
from jax.experimental import pallas as pl
from jax.experimental.pallas import tpu as pltpu
from jax.sharding import Mesh, PartitionSpec as P

ROW, COL = ("x_hi", "z"), ("y", "x_lo")
PLAIN = (((1,), (0,)), ((), ()))
LAST = (((1,), (1,)), ((), ()))
FIRST = (((0,), (0,)), ((), ()))
SWAP = [(0, 1), (1, 0)]
f32, bf16 = jnp.float32, jnp.bfloat16


def swiglu_back(gate, up, grad_hidden):
    sig = jax.nn.sigmoid(gate)
    hidden = (gate * sig * up).astype(bf16)
    grad_g = (grad_hidden * up * sig * (1.0 + gate * (1.0 - sig))).astype(bf16)
    grad_u = (grad_hidden * gate * sig).astype(bf16)
    return hidden, grad_g, grad_u


def dot(a, b, dims):
    return lax.dot_general(a, b, dims, preferred_element_type=f32)


Z_ORDER = (0, 4, 7, 3, 1, 5, 6, 2)
COL_ORDER = (7, 0, 6, 2, 14, 12, 15, 8, 13, 4, 1, 9, 3, 11, 10, 5)


def exchange(x, axis):
    order = Z_ORDER if axis == "z" else COL_ORDER
    return lax.all_to_all(x, axis, 0, 0, tiled=True, axis_index_groups=[list(order)])


def gather(x, axis, n):
    rows, cols = x.shape
    copies = jnp.broadcast_to(x[None], (n, rows, cols))
    return exchange(copies, axis).reshape(n * rows, cols)


def scatter_sum(x, axis, n):
    rows, cols = x.shape
    return jnp.sum(exchange(x.reshape(n, rows // n, cols), axis).astype(f32), axis=0)


def gate_up_grads_kernel(x_hi, own, other, own_gu, far_gu, other_own, other_far, gate_ref, up_ref):
    def part(mine, others):
        total = dot(own[...], mine[:, :512], FIRST) + dot(other[...], others[...], FIRST)
        gate_ref[...] = total[:, :256].astype(bf16)
        up_ref[...] = total[:, 256:].astype(bf16)

    pl.when(pl.program_id(0) == 0)(lambda: part(own_gu, other_own))
    pl.when(pl.program_id(0) == 1)(lambda: part(far_gu, other_far))


def gate_up_grads(x_hi, own, other, own_gu, far_gu, other_own, other_far):
    whole = lambda shape: pl.BlockSpec(shape, lambda q, at: (0, 0))
    out = pl.BlockSpec((512, 256), lambda q, at: (0, at[0] ^ q))
    shape = jax.ShapeDtypeStruct((512, 512), bf16)
    return pl.pallas_call(
        gate_up_grads_kernel,
        out_shape=(shape, shape),
        grid_spec=pltpu.PrefetchScalarGridSpec(
            num_scalar_prefetch=1,
            grid=(2,),
            in_specs=[whole((256, 512)), whole((256, 512)), whole((256, 1024)), whole((256, 1024)),
                      whole((256, 512)), whole((256, 512))],
            out_specs=(out, out),
        ),
        compiler_params=pltpu.CompilerParams(vmem_limit_bytes=24 * 2**20),
        cost_estimate=pl.CostEstimate(flops=2 * 512**3 * 2, bytes_accessed=4 * 2**20, transcendentals=0),
    )(x_hi, own, other, own_gu, far_gu, other_own, other_far)


def down_grads_kernel(x_hi, own, other, own_h, far_h, out_ref):
    def part(h):
        total = dot(h[:, :256], own[...], FIRST) + dot(h[:, 256:], other[...], FIRST)
        out_ref[...] = total.astype(bf16)

    pl.when(pl.program_id(0) == 0)(lambda: part(own_h))
    pl.when(pl.program_id(0) == 1)(lambda: part(far_h))


def down_grads(x_hi, own, other, own_h, far_h):
    half = lambda column: pl.BlockSpec((256, 512), lambda q, at: (0, column))
    return pl.pallas_call(
        down_grads_kernel,
        out_shape=jax.ShapeDtypeStruct((512, 512), bf16),
        grid_spec=pltpu.PrefetchScalarGridSpec(
            num_scalar_prefetch=1,
            grid=(2,),
            in_specs=[half(1), half(1), half(0), half(0)],
            out_specs=pl.BlockSpec((256, 512), lambda q, at: (at[0] ^ q, 0)),
        ),
        compiler_params=pltpu.CompilerParams(vmem_limit_bytes=24 * 2**20),
        cost_estimate=pl.CostEstimate(flops=2 * 512**3, bytes_accessed=2 * 2**20, transcendentals=0),
    )(x_hi, own, other, own_h, far_h)


def body(tokens, grad_out, gate_weight, up_weight, down_weight):
    x_hi, dp = lax.axis_index("x_hi"), lax.axis_index("dp")
    def quarter(x, core, side):
        return lax.dynamic_slice(x, (0, core * 512 + side * 256), (x.shape[0], 256))

    def gate_up(side):
        return jnp.concatenate(
            [quarter(w, core, side) for core in (dp, 1 - dp) for w in (gate_weight, up_weight)], axis=1
        )

    gu_keep, gu_send = gate_up(x_hi), gate_up(1 - x_hi)
    own = gather(jnp.concatenate([tokens, grad_out], axis=1), COL, 16)
    own, gu_keep, gu_send = lax.optimization_barrier((own, gu_keep, gu_send))
    own_in, own_grad = own[:, :512], own[:, 512:]

    got = lax.ppermute(dot(own_in, gu_send, PLAIN).astype(bf16), "x_hi", SWAP)
    gh_part = scatter_sum(dot(own_grad, down_weight, LAST).astype(bf16), "z", 8)

    def grad_hidden(side):
        return jnp.concatenate([quarter(gh_part, dp, side), quarter(gh_part, 1 - dp, side)], axis=1)

    gh = grad_hidden(x_hi) + lax.ppermute(grad_hidden(1 - x_hi), "x_hi", SWAP)
    other = lax.ppermute(own, "dp", SWAP)
    kept = lax.optimization_barrier(dot(own_in, gu_keep, PLAIN))
    got, other = lax.optimization_barrier((got, other))
    gu = scatter_sum((kept + got.astype(f32)).astype(bf16), "z", 8)
    gate = jnp.concatenate([gu[:, :256], gu[:, 512:768]], axis=1)
    up = jnp.concatenate([gu[:, 256:512], gu[:, 768:]], axis=1)
    hidden, g, u = swiglu_back(gate, up, gh)

    own_gu = gather(jnp.concatenate([g[:, :256], u[:, :256], g[:, 256:], u[:, 256:]], axis=1), "z", 8)
    hidden = jnp.concatenate([hidden[:, :256], lax.ppermute(hidden[:, 256:], "dp", SWAP)], axis=1)
    copies = jnp.broadcast_to(hidden[None], (8, 32, 512))
    own_gu, copies = lax.optimization_barrier((own_gu, copies))
    own_h = exchange(copies, "z").reshape(256, 512)
    far_h = lax.ppermute(own_h, "x_hi", SWAP)

    far_gu = lax.ppermute(own_gu, "x_hi", SWAP)
    kept = lax.optimization_barrier(dot(own_gu, gu_keep, LAST))
    panel = (kept + dot(far_gu, gu_send, LAST)).astype(bf16)
    panel, far_gu, own_gu = lax.optimization_barrier((panel, far_gu, own_gu))
    grad_tokens = scatter_sum(panel, COL, 16).astype(bf16)

    other_own = lax.ppermute(own_gu[:, 512:], "dp", SWAP)
    other_far = lax.ppermute(far_gu[:, 512:], "dp", SWAP)
    at = x_hi.astype(jnp.int32)[None]
    grad_gate, grad_up = gate_up_grads(
        at, own, other, own_gu, far_gu, other_own, other_far
    )
    grad_down = down_grads(at, own, other, own_h, far_h)
    return grad_tokens, grad_gate, grad_up, grad_down


def solution(mesh):
    fine = Mesh(mesh.devices.reshape(2, 8, 8, 2, 2), ("x_hi", "z", "y", "x_lo", "dp"))
    in_specs = (
        P(COL + ("dp",), ROW),
        P(COL + ("dp",), ROW),
        P(ROW, COL),
        P(ROW, COL),
        P(COL, ROW),
    )
    out_specs = (
        P(COL + ("dp",), ROW),
        P(ROW, COL + ("dp",)),
        P(ROW, COL + ("dp",)),
        P(COL + ("dp",), ROW),
    )
    return jax.shard_map(body, mesh=fine, in_specs=in_specs, out_specs=out_specs, check_vma=False)
```

```python
import jax
import jax.numpy as jnp
from jax import lax
from jax.experimental import pallas as pl
from jax.experimental.pallas import tpu as pltpu
from jax.sharding import Mesh, PartitionSpec as P

ROW, COL = ("x_hi", "z"), ("y", "x_lo")
PLAIN = (((1,), (0,)), ((), ()))
LAST = (((1,), (1,)), ((), ()))
FIRST = (((0,), (0,)), ((), ()))
SWAP = [(0, 1), (1, 0)]
f32, bf16 = jnp.float32, jnp.bfloat16


def swiglu_back(gate, up, grad_hidden):
    sig = jax.nn.sigmoid(gate)
    hidden = (gate * sig * up).astype(bf16)
    grad_g = (grad_hidden * up * sig * (1.0 + gate * (1.0 - sig))).astype(bf16)
    grad_u = (grad_hidden * gate * sig).astype(bf16)
    return hidden, grad_g, grad_u


def dot(a, b, dims):
    return lax.dot_general(a, b, dims, preferred_element_type=f32)


Z_ORDER = (0, 4, 7, 3, 1, 5, 6, 2)
COL_ORDER = (15, 1, 0, 4, 6, 5, 11, 3, 12, 13, 2, 7, 14, 10, 8, 9)


def exchange(x, axis):
    order = Z_ORDER if axis == "z" else COL_ORDER
    return lax.all_to_all(x, axis, 0, 0, tiled=True, axis_index_groups=[list(order)])


def gather(x, axis, n):
    rows, cols = x.shape
    copies = jnp.broadcast_to(x[None], (n, rows, cols))
    return exchange(copies, axis).reshape(n * rows, cols)


def scatter_sum(x, axis, n):
    rows, cols = x.shape
    return jnp.sum(exchange(x.reshape(n, rows // n, cols), axis).astype(f32), axis=0)


def weight_grads_kernel(
    x_hi, own, other, own_gu, far_gu, other_own, other_far, own_h, far_h,
    gate_ref, up_ref, down_ref,
):
    def part(mine, others, h):
        total = dot(own[:, :512], mine[:, :512], FIRST) + dot(other[:, :512], others[...], FIRST)
        gate_ref[...] = total[:, :256].astype(bf16)
        up_ref[...] = total[:, 256:].astype(bf16)
        total = dot(h[:, :256], own[:, 512:], FIRST) + dot(h[:, 256:], other[:, 512:], FIRST)
        down_ref[...] = total.astype(bf16)

    pl.when(pl.program_id(0) == 0)(lambda: part(own_gu, other_own, own_h))
    pl.when(pl.program_id(0) == 1)(lambda: part(far_gu, other_far, far_h))


def weight_grads(*args):
    whole = lambda x: pl.BlockSpec(x.shape, lambda q, at: (0,) * x.ndim)
    columns = pl.BlockSpec((512, 256), lambda q, at: (0, at[0] ^ q))
    rows = pl.BlockSpec((256, 512), lambda q, at: (at[0] ^ q, 0))
    weight = jax.ShapeDtypeStruct((512, 512), bf16)
    return pl.pallas_call(
        weight_grads_kernel,
        out_shape=(weight, weight, weight),
        grid_spec=pltpu.PrefetchScalarGridSpec(
            num_scalar_prefetch=1,
            grid=(2,),
            in_specs=[whole(x) for x in args[1:]],
            out_specs=(columns, columns, rows),
        ),
        compiler_params=pltpu.CompilerParams(vmem_limit_bytes=24 * 2**20),
        cost_estimate=pl.CostEstimate(flops=6 * 512**3, bytes_accessed=5 * 2**20, transcendentals=0),
    )(*args)


def body(tokens, grad_out, gate_weight, up_weight, down_weight):
    x_hi, dp = lax.axis_index("x_hi"), lax.axis_index("dp")
    def quarter(x, core, side):
        return lax.dynamic_slice(x, (0, core * 512 + side * 256), (x.shape[0], 256))

    def gate_up(side):
        return jnp.concatenate(
            [quarter(w, core, side) for core in (dp, 1 - dp) for w in (gate_weight, up_weight)], axis=1
        )

    gu_keep, gu_send = gate_up(x_hi), gate_up(1 - x_hi)
    own = gather(jnp.concatenate([tokens, grad_out], axis=1), COL, 16)
    own, gu_keep, gu_send = lax.optimization_barrier((own, gu_keep, gu_send))
    own_in, own_grad = own[:, :512], own[:, 512:]

    got = lax.ppermute(dot(own_in, gu_send, PLAIN).astype(bf16), "x_hi", SWAP)
    gh_part = scatter_sum(dot(own_grad, down_weight, LAST).astype(bf16), "z", 8)

    def grad_hidden(side):
        return jnp.concatenate([quarter(gh_part, dp, side), quarter(gh_part, 1 - dp, side)], axis=1)

    gh = grad_hidden(x_hi) + lax.ppermute(grad_hidden(1 - x_hi), "x_hi", SWAP)
    other = lax.ppermute(own, "dp", SWAP)
    kept = lax.optimization_barrier(dot(own_in, gu_keep, PLAIN))
    got, other = lax.optimization_barrier((got, other))
    gu = scatter_sum((kept + got.astype(f32)).astype(bf16), "z", 8)
    gate = jnp.concatenate([gu[:, :256], gu[:, 512:768]], axis=1)
    up = jnp.concatenate([gu[:, 256:512], gu[:, 768:]], axis=1)
    hidden, g, u = swiglu_back(gate, up, gh)

    own_gu = gather(jnp.concatenate([g[:, :256], u[:, :256], g[:, 256:], u[:, 256:]], axis=1), "z", 8)
    hidden = jnp.concatenate([hidden[:, :256], lax.ppermute(hidden[:, 256:], "dp", SWAP)], axis=1)
    copies = jnp.broadcast_to(hidden[None], (8, 32, 512))
    own_gu, copies = lax.optimization_barrier((own_gu, copies))
    own_h = exchange(copies, "z").reshape(256, 512)
    far_h = lax.ppermute(own_h, "x_hi", SWAP)

    far_gu = lax.ppermute(own_gu, "x_hi", SWAP)
    kept = lax.optimization_barrier(dot(own_gu, gu_keep, LAST))
    panel = (kept + dot(far_gu, gu_send, LAST)).astype(bf16)
    panel, far_gu, own_gu = lax.optimization_barrier((panel, far_gu, own_gu))
    grad_tokens = scatter_sum(panel, COL, 16).astype(bf16)

    other_own = lax.ppermute(own_gu[:, 512:], "dp", SWAP)
    other_far = lax.ppermute(far_gu[:, 512:], "dp", SWAP)
    at = x_hi.astype(jnp.int32)[None]
    grad_gate, grad_up, grad_down = weight_grads(
        at, own, other, own_gu, far_gu, other_own, other_far, own_h, far_h
    )
    return grad_tokens, grad_gate, grad_up, grad_down


def solution(mesh):
    fine = Mesh(mesh.devices.reshape(2, 8, 8, 2, 2), ("x_hi", "z", "y", "x_lo", "dp"))
    in_specs = (
        P(COL + ("dp",), ROW),
        P(COL + ("dp",), ROW),
        P(ROW, COL),
        P(ROW, COL),
        P(COL, ROW),
    )
    out_specs = (
        P(COL + ("dp",), ROW),
        P(ROW, COL + ("dp",)),
        P(ROW, COL + ("dp",)),
        P(COL + ("dp",), ROW),
    )
    return jax.shard_map(body, mesh=fine, in_specs=in_specs, out_specs=out_specs, check_vma=False)
```

```python
import jax
import jax.numpy as jnp
from jax import lax
from jax.experimental import pallas as pl
from jax.experimental.pallas import tpu as pltpu
from jax.sharding import Mesh, PartitionSpec as P

ROW, COL = ("x_hi", "z"), ("y", "x_lo")
PLAIN = (((1,), (0,)), ((), ()))
LAST = (((1,), (1,)), ((), ()))
FIRST = (((0,), (0,)), ((), ()))
SWAP = [(0, 1), (1, 0)]
f32, bf16 = jnp.float32, jnp.bfloat16


def swiglu_back(gate, up, grad_hidden):
    sig = jax.nn.sigmoid(gate)
    hidden = (gate * sig * up).astype(bf16)
    grad_g = (grad_hidden * up * sig * (1.0 + gate * (1.0 - sig))).astype(bf16)
    grad_u = (grad_hidden * gate * sig).astype(bf16)
    return hidden, grad_g, grad_u


def dot(a, b, dims):
    return lax.dot_general(a, b, dims, preferred_element_type=f32)


Z_ORDER = (0, 4, 7, 3, 1, 5, 6, 2)
COL_ORDER = (0, 2, 4, 6, 8, 10, 12, 14, 1, 3, 5, 7, 9, 11, 13, 15)


def exchange(x, axis):
    order = Z_ORDER if axis == "z" else COL_ORDER
    return lax.all_to_all(x, axis, 0, 0, tiled=True, axis_index_groups=[list(order)])


def gather(x, axis, n):
    rows, cols = x.shape
    copies = jnp.broadcast_to(x[None], (n, rows, cols))
    return exchange(copies, axis).reshape(n * rows, cols)


def scatter_sum(x, axis, n):
    rows, cols = x.shape
    return jnp.sum(exchange(x.reshape(n, rows // n, cols), axis).astype(f32), axis=0)


def weight_grads_kernel(
    x_hi, own, other, own_gu, far_gu, other_own, other_far, own_h, far_h,
    gate_ref, up_ref, down_ref,
):
    def part(mine, others, h):
        total = dot(own[:, :512], mine[:, :512], FIRST) + dot(other[:, :512], others[...], FIRST)
        gate_ref[...] = total[:, :256].astype(bf16)
        up_ref[...] = total[:, 256:].astype(bf16)
        total = dot(h[:, :256], own[:, 512:], FIRST) + dot(h[:, 256:], other[:, 512:], FIRST)
        down_ref[...] = total.astype(bf16)

    pl.when(pl.program_id(0) == 0)(lambda: part(own_gu, other_own, own_h))
    pl.when(pl.program_id(0) == 1)(lambda: part(far_gu, other_far, far_h))


def weight_grads(*args):
    whole = lambda x: pl.BlockSpec(x.shape, lambda q, at: (0,) * x.ndim)
    columns = pl.BlockSpec((512, 256), lambda q, at: (0, at[0] ^ q))
    rows = pl.BlockSpec((256, 512), lambda q, at: (at[0] ^ q, 0))
    weight = jax.ShapeDtypeStruct((512, 512), bf16)
    return pl.pallas_call(
        weight_grads_kernel,
        out_shape=(weight, weight, weight),
        grid_spec=pltpu.PrefetchScalarGridSpec(
            num_scalar_prefetch=1,
            grid=(2,),
            in_specs=[whole(x) for x in args[1:]],
            out_specs=(columns, columns, rows),
        ),
        compiler_params=pltpu.CompilerParams(vmem_limit_bytes=24 * 2**20),
        cost_estimate=pl.CostEstimate(flops=6 * 512**3, bytes_accessed=5 * 2**20, transcendentals=0),
    )(*args)


def body(tokens, grad_out, gate_weight, up_weight, down_weight):
    x_hi, dp = lax.axis_index("x_hi"), lax.axis_index("dp")
    def quarter(x, core, side):
        return lax.dynamic_slice(x, (0, core * 512 + side * 256), (x.shape[0], 256))

    def gate_up(side):
        return jnp.concatenate(
            [quarter(w, core, side) for core in (dp, 1 - dp) for w in (gate_weight, up_weight)], axis=1
        )

    gu_keep, gu_send = gate_up(x_hi), gate_up(1 - x_hi)
    own = gather(jnp.concatenate([tokens, grad_out], axis=1), COL, 16)
    own, gu_keep, gu_send = lax.optimization_barrier((own, gu_keep, gu_send))
    own_in, own_grad = own[:, :512], own[:, 512:]

    got = lax.ppermute(dot(own_in, gu_send, PLAIN).astype(bf16), "x_hi", SWAP)
    gh_part = scatter_sum(dot(own_grad, down_weight, LAST).astype(bf16), "z", 8)

    def grad_hidden(side):
        return jnp.concatenate([quarter(gh_part, dp, side), quarter(gh_part, 1 - dp, side)], axis=1)

    gh = grad_hidden(x_hi) + lax.ppermute(grad_hidden(1 - x_hi), "x_hi", SWAP)
    other = lax.ppermute(own, "dp", SWAP)
    kept = lax.optimization_barrier(dot(own_in, gu_keep, PLAIN))
    got, other = lax.optimization_barrier((got, other))
    gu = scatter_sum((kept + got.astype(f32)).astype(bf16), "z", 8)
    gate = jnp.concatenate([gu[:, :256], gu[:, 512:768]], axis=1)
    up = jnp.concatenate([gu[:, 256:512], gu[:, 768:]], axis=1)
    hidden, g, u = swiglu_back(gate, up, gh)

    own_gu = gather(jnp.concatenate([g[:, :256], u[:, :256], g[:, 256:], u[:, 256:]], axis=1), "z", 8)
    hidden = jnp.concatenate([hidden[:, :256], lax.ppermute(hidden[:, 256:], "dp", SWAP)], axis=1)
    copies = jnp.broadcast_to(hidden[None], (8, 32, 512))
    own_gu, copies = lax.optimization_barrier((own_gu, copies))
    own_h = exchange(copies, "z").reshape(256, 512)
    far_h = lax.ppermute(own_h, "x_hi", SWAP)

    far_gu = lax.ppermute(own_gu, "x_hi", SWAP)
    kept = lax.optimization_barrier(dot(own_gu, gu_keep, LAST))
    panel = (kept + dot(far_gu, gu_send, LAST)).astype(bf16)
    panel, far_gu, own_gu = lax.optimization_barrier((panel, far_gu, own_gu))
    grad_tokens = scatter_sum(panel, COL, 16).astype(bf16)

    other_own = lax.ppermute(own_gu[:, 512:], "dp", SWAP)
    other_far = lax.ppermute(far_gu[:, 512:], "dp", SWAP)
    at = x_hi.astype(jnp.int32)[None]
    grad_gate, grad_up, grad_down = weight_grads(
        at, own, other, own_gu, far_gu, other_own, other_far, own_h, far_h
    )
    return grad_tokens, grad_gate, grad_up, grad_down


def solution(mesh):
    fine = Mesh(mesh.devices.reshape(2, 8, 8, 2, 2), ("x_hi", "z", "y", "x_lo", "dp"))
    in_specs = (
        P(COL + ("dp",), ROW),
        P(COL + ("dp",), ROW),
        P(ROW, COL),
        P(ROW, COL),
        P(COL, ROW),
    )
    out_specs = (
        P(COL + ("dp",), ROW),
        P(ROW, COL + ("dp",)),
        P(ROW, COL + ("dp",)),
        P(COL + ("dp",), ROW),
    )
    return jax.shard_map(body, mesh=fine, in_specs=in_specs, out_specs=out_specs, check_vma=False)
```

```python
import jax
import jax.numpy as jnp
from jax import lax
from jax.experimental import pallas as pl
from jax.experimental.pallas import tpu as pltpu
from jax.sharding import Mesh, PartitionSpec as P

ROW, COL = ("x_hi", "z"), ("y", "x_lo")
PLAIN = (((1,), (0,)), ((), ()))
LAST = (((1,), (1,)), ((), ()))
FIRST = (((0,), (0,)), ((), ()))
SWAP = [(0, 1), (1, 0)]
f32, bf16 = jnp.float32, jnp.bfloat16


def swiglu_back(gate, up, grad_hidden):
    sig = jax.nn.sigmoid(gate)
    hidden = (gate * sig * up).astype(bf16)
    grad_g = (grad_hidden * up * sig * (1.0 + gate * (1.0 - sig))).astype(bf16)
    grad_u = (grad_hidden * gate * sig).astype(bf16)
    return hidden, grad_g, grad_u


def dot(a, b, dims):
    return lax.dot_general(a, b, dims, preferred_element_type=f32)


Z_ORDER = (0, 4, 6, 7, 2, 5, 1, 3)
COL_ORDER = (0, 2, 4, 6, 8, 10, 12, 14, 1, 3, 5, 7, 9, 11, 13, 15)


def exchange(x, axis):
    order = Z_ORDER if axis == "z" else COL_ORDER
    return lax.all_to_all(x, axis, 0, 0, tiled=True, axis_index_groups=[list(order)])


def gather(x, axis, n):
    rows, cols = x.shape
    copies = jnp.broadcast_to(x[None], (n, rows, cols))
    return exchange(copies, axis).reshape(n * rows, cols)


def scatter_sum(x, axis, n):
    rows, cols = x.shape
    return jnp.sum(exchange(x.reshape(n, rows // n, cols), axis).astype(f32), axis=0)


def weight_grads_kernel(
    x_hi, own, other, own_gu, far_gu, other_own, other_far, own_h, far_h,
    gate_ref, up_ref, down_ref,
):
    def part(mine, others, h):
        total = dot(own[:, :512], mine[:, :512], FIRST) + dot(other[:, :512], others[...], FIRST)
        gate_ref[...] = total[:, :256].astype(bf16)
        up_ref[...] = total[:, 256:].astype(bf16)
        total = dot(h[:, :256], own[:, 512:], FIRST) + dot(h[:, 256:], other[:, 512:], FIRST)
        down_ref[...] = total.astype(bf16)

    pl.when(pl.program_id(0) == 0)(lambda: part(own_gu, other_own, own_h))
    pl.when(pl.program_id(0) == 1)(lambda: part(far_gu, other_far, far_h))


def weight_grads(*args):
    whole = lambda x: pl.BlockSpec(x.shape, lambda q, at: (0,) * x.ndim)
    columns = pl.BlockSpec((512, 256), lambda q, at: (0, at[0] ^ q))
    rows = pl.BlockSpec((256, 512), lambda q, at: (at[0] ^ q, 0))
    weight = jax.ShapeDtypeStruct((512, 512), bf16)
    return pl.pallas_call(
        weight_grads_kernel,
        out_shape=(weight, weight, weight),
        grid_spec=pltpu.PrefetchScalarGridSpec(
            num_scalar_prefetch=1,
            grid=(2,),
            in_specs=[whole(x) for x in args[1:]],
            out_specs=(columns, columns, rows),
        ),
        compiler_params=pltpu.CompilerParams(vmem_limit_bytes=24 * 2**20),
        cost_estimate=pl.CostEstimate(flops=6 * 512**3, bytes_accessed=5 * 2**20, transcendentals=0),
    )(*args)


def body(tokens, grad_out, gate_weight, up_weight, down_weight):
    x_hi, dp = lax.axis_index("x_hi"), lax.axis_index("dp")
    def quarter(x, core, side):
        return lax.dynamic_slice(x, (0, core * 512 + side * 256), (x.shape[0], 256))

    def gate_up(side):
        return jnp.concatenate(
            [quarter(w, core, side) for core in (dp, 1 - dp) for w in (gate_weight, up_weight)], axis=1
        )

    gu_keep, gu_send = gate_up(x_hi), gate_up(1 - x_hi)
    own = gather(jnp.concatenate([tokens, grad_out], axis=1), COL, 16)
    own, gu_keep, gu_send = lax.optimization_barrier((own, gu_keep, gu_send))
    own_in, own_grad = own[:, :512], own[:, 512:]

    got = lax.ppermute(dot(own_in, gu_send, PLAIN).astype(bf16), "x_hi", SWAP)
    gh_part = scatter_sum(dot(own_grad, down_weight, LAST).astype(bf16), "z", 8)

    def grad_hidden(side):
        return jnp.concatenate([quarter(gh_part, dp, side), quarter(gh_part, 1 - dp, side)], axis=1)

    gh = grad_hidden(x_hi) + lax.ppermute(grad_hidden(1 - x_hi), "x_hi", SWAP)
    other = lax.ppermute(own, "dp", SWAP)
    kept = lax.optimization_barrier(dot(own_in, gu_keep, PLAIN))
    got, other = lax.optimization_barrier((got, other))
    gu = scatter_sum((kept + got.astype(f32)).astype(bf16), "z", 8)
    gate = jnp.concatenate([gu[:, :256], gu[:, 512:768]], axis=1)
    up = jnp.concatenate([gu[:, 256:512], gu[:, 768:]], axis=1)
    hidden, g, u = swiglu_back(gate, up, gh)

    own_gu = gather(jnp.concatenate([g[:, :256], u[:, :256], g[:, 256:], u[:, 256:]], axis=1), "z", 8)
    hidden = jnp.concatenate([hidden[:, :256], lax.ppermute(hidden[:, 256:], "dp", SWAP)], axis=1)
    copies = jnp.broadcast_to(hidden[None], (8, 32, 512))
    own_gu, copies = lax.optimization_barrier((own_gu, copies))
    own_h = exchange(copies, "z").reshape(256, 512)
    far_h = lax.ppermute(own_h, "x_hi", SWAP)

    far_gu = lax.ppermute(own_gu, "x_hi", SWAP)
    kept = lax.optimization_barrier(dot(own_gu, gu_keep, LAST))
    panel = (kept + dot(far_gu, gu_send, LAST)).astype(bf16)
    panel, far_gu, own_gu = lax.optimization_barrier((panel, far_gu, own_gu))
    grad_tokens = scatter_sum(panel, COL, 16).astype(bf16)

    other_own = lax.ppermute(own_gu[:, 512:], "dp", SWAP)
    other_far = lax.ppermute(far_gu[:, 512:], "dp", SWAP)
    at = x_hi.astype(jnp.int32)[None]
    grad_gate, grad_up, grad_down = weight_grads(
        at, own, other, own_gu, far_gu, other_own, other_far, own_h, far_h
    )
    return grad_tokens, grad_gate, grad_up, grad_down


def solution(mesh):
    fine = Mesh(mesh.devices.reshape(2, 8, 8, 2, 2), ("x_hi", "z", "y", "x_lo", "dp"))
    in_specs = (
        P(COL + ("dp",), ROW),
        P(COL + ("dp",), ROW),
        P(ROW, COL),
        P(ROW, COL),
        P(COL, ROW),
    )
    out_specs = (
        P(COL + ("dp",), ROW),
        P(ROW, COL + ("dp",)),
        P(ROW, COL + ("dp",)),
        P(COL + ("dp",), ROW),
    )
    return jax.shard_map(body, mesh=fine, in_specs=in_specs, out_specs=out_specs, check_vma=False)
```
